32 devices in a mesh: node: 8 (over y, x, core), local: 4 (over z).
Axes of the slice: x: 2, y: 2, z: 4, core: 2. Of those that a mesh axis runs over, the one named last changes fastest.
Arguments:
- upstream: bfloat16 [256, 12800], P(('node', 'local')), may hold values from -1.5 to 1.5
- block_image: int32 [64], replicated, may hold values from 0 to 15, as said below
- image_owner: int32 [16], replicated, may hold values from 0 to 7, as said below
- vision_out: bfloat16 [24, 4, 12800], P('node', 'local'), may hold values from -200 to 200
- norm_gain: float32 [12800], replicated, may hold values from 0.5 to 2
- layer_scale: float32 [3200], replicated, may hold values from 0.5 to 2
- down_weight: bfloat16 [3200, 2144], P(None, 'local'), may hold values from -0.125 to 0.125
- hidden_pre: bfloat16 [24, 16, 2144], P('node', None, 'local'), may hold values from -6 to 6
Outputs:
- hidden_grad: bfloat16 [24, 16, 2144], P('node', None, 'local')
- down_grad: float32 [3200, 2144], P('node', 'local')
- norm_grads: float32 [2, 12800], replicated
The draws below stay inside these ranges and needn't reach their ends.
Inputs may be any that keep to these rules, and one draw needn't show every extreme that they name: `block_image`: within one node's blocks, images with the same owner are the same image, so a node reads at most one image of each owner; an image may be read by several blocks of a node and by several nodes. `image_owner`: every node owns at least one image and at most 3, and some node owns exactly 3.
All inputs are finite; a program needn't handle non-finite values.
Results may differ from the reference program's by a relative error of at most 0.0057.
Values may be sent and summed in bfloat16 or wider, within the bound.
A program may use at most 64 MiB of HBM per device.

```python
import math
import jax
import jax.numpy as jnp
from jax import lax

DV = 3200
BLOCKS = 2
IMG_NODE = 2
IMG_TOK = 4
PATCH_IMG = 16
D_IN = 12800
FFV = 2144
OWN_CAP = 3
NIMG = 16
SLOTS = 24
ROWS = 8
N_NODE = 8
N_LOCAL = 4


def owner_draw(key):
    key = jax.random.fold_in(key, 11)
    order_key, split_key, place_key = jax.random.split(key, 3)
    half_nodes = N_NODE // 2
    paired = jax.random.permutation(order_key, N_NODE)
    shifts = jax.random.randint(split_key, (half_nodes,), 0, IMG_NODE)
    shifts = shifts.at[0].set(IMG_NODE - 1)
    counts = jnp.zeros((N_NODE,), jnp.int32)
    counts = counts.at[paired[:half_nodes]].set(IMG_NODE + shifts)
    counts = counts.at[paired[half_nodes:]].set(IMG_NODE - shifts)
    bounds = jnp.cumsum(counts)
    sorted_owner = jnp.searchsorted(bounds, jnp.arange(NIMG, dtype=jnp.int32), side='right').astype(jnp.int32)
    return jax.random.permutation(place_key, sorted_owner).astype(jnp.int32)


def draw_image_owner(key, part):
    return owner_draw(key)


def draw_block_image(key, part):
    image_owner = owner_draw(key)
    key = jax.random.fold_in(key, 23)
    pick_key, choose_key = jax.random.split(key, 2)
    by_owner = jnp.argsort(image_owner, stable=True).astype(jnp.int32)
    node_table = jnp.arange(N_NODE, dtype=jnp.int32)
    counts = jnp.sum((image_owner[None, :] == node_table[:, None]).astype(jnp.int32), axis=1)
    starts = jnp.cumsum(counts) - counts
    choose = jax.random.randint(choose_key, (N_NODE, N_NODE), 0, 1 << 20) % counts[None, :]
    chosen = by_owner[starts[None, :] + choose]
    wanted = jax.random.randint(pick_key, (N_NODE, N_LOCAL * BLOCKS), 0, NIMG)
    wanted_owner = image_owner[wanted]
    result = jnp.take_along_axis(chosen, wanted_owner, axis=1)
    return result.reshape(-1).astype(jnp.int32)


def draw_vision_out(key, part):
    key = jax.random.fold_in(key, 37)
    base_key, scale_key, shift_key, column_key = jax.random.split(key, 4)
    full_shape = (SLOTS, IMG_TOK, D_IN)
    column_scale = jnp.exp(jax.random.uniform(column_key, (D_IN,), minval=-0.69, maxval=0.69))
    values = jax.random.truncated_normal(base_key, -3.0, 3.0, full_shape) * column_scale
    row_scale = jnp.exp(jax.random.uniform(scale_key, (SLOTS, IMG_TOK, 1), minval=0.0, maxval=2.3))
    row_shift = jax.random.uniform(shift_key, (SLOTS, IMG_TOK, 1), minval=-2.0, maxval=2.0)
    return ((values + row_shift) * row_scale).astype(jnp.bfloat16)


def steps_of(key, shape, cuts, low, high):
    loudness = 1.0
    for dim, shards_of in cuts:
        heights = jax.random.uniform(jax.random.fold_in(jax.random.fold_in(key, 6), dim), (shards_of,), jnp.float32, low / len(cuts), high / len(cuts))
        loudness = loudness * jnp.repeat(jnp.exp(heights), shape[dim] // shards_of).reshape((-1,) + (1,) * (len(shape) - 1 - dim))
    return loudness


def bell_draw(rng, shape, width, bound, shards=(), kind=jnp.bfloat16):
    drawn = width * jax.random.normal(rng, shape, jnp.float32)
    if shards:
        drawn = drawn * steps_of(rng, shape, shards, -0.22, 0.18)
    return jnp.clip(drawn, -bound, bound).astype(kind)


def setup_inputs(seed: int = 0) -> dict:
    seeds = jax.random.split(jax.random.key(seed), 9)
    return {
        "upstream": bell_draw(seeds[0], (N_NODE * N_LOCAL * ROWS, D_IN), 0.25, 1.5, ((0, 32),)),
        "block_image": draw_block_image(jax.random.fold_in(seeds[8], 71), 0),
        "image_owner": draw_image_owner(jax.random.fold_in(seeds[8], 71), 0),
        "vision_out": draw_vision_out(jax.random.fold_in(seeds[8], 71), 0),
        "norm_gain": jnp.clip(jnp.exp(jax.random.uniform(seeds[4], (D_IN,), jnp.float32, math.log(0.5), math.log(2.0))), 0.5, 2.0),
        "layer_scale": jnp.clip(jnp.exp(jax.random.uniform(seeds[5], (DV,), jnp.float32, math.log(0.5), math.log(2.0))), 0.5, 2.0),
        "down_weight": bell_draw(seeds[6], (DV, FFV), FFV ** -0.5, 0.125, ((1, 4),)),
        "hidden_pre": bell_draw(seeds[7], (SLOTS, PATCH_IMG, FFV), 1.0, 6.0, ((0, 8), (2, 4))),
    }


epsilon = 1e-06
half_root = 0.7071067811865476
inv_root_two_pi = 0.3989422804014327

def gelu_parts(preact):
    normal_cdf = 0.5 * (1.0 + jax.scipy.special.erf(preact * half_root))
    density = jnp.exp(-0.5 * preact * preact) * inv_root_two_pi
    return (preact * normal_cdf, normal_cdf + preact * density)

def owner_ranks(image_owner):
    positions = jnp.arange(image_owner.shape[0], dtype=jnp.int32)
    same_owner = (image_owner[:, None] == image_owner[None, :]) & (positions[None, :] < positions[:, None])
    return lax.optimization_barrier(jnp.sum(same_owner.astype(jnp.int32), axis=1)).astype(jnp.int32)

def reference(upstream, block_image, image_owner, vision_out, norm_gain, layer_scale, down_weight, hidden_pre):
    node_blocks = N_LOCAL * BLOCKS
    all_rows = upstream.reshape(N_NODE, node_blocks, IMG_TOK * D_IN)
    all_ids = block_image.reshape(N_NODE, node_blocks)
    images = jnp.arange(NIMG, dtype=jnp.int32)

    def add_node(image_sum, entry):
        node_rows, node_ids = entry
        member = (images[:, None] == node_ids[None, :]).astype(jnp.bfloat16)
        node_sum = jnp.dot(member, node_rows, preferred_element_type=jnp.float32)
        rounded = lax.optimization_barrier(node_sum.astype(jnp.bfloat16))
        return (image_sum + rounded.astype(jnp.float32), None)
    start_sum = jnp.zeros((NIMG, IMG_TOK * D_IN), jnp.float32)
    image_sum, ignored = lax.scan(add_node, start_sum, (all_rows, all_ids))
    slot_index = (image_owner * OWN_CAP + owner_ranks(image_owner)).astype(jnp.int32)
    slot_grad = jnp.zeros((SLOTS, IMG_TOK * D_IN), jnp.float32).at[slot_index].set(image_sum)
    grad_rows = slot_grad.reshape(SLOTS * IMG_TOK, D_IN)
    inputs = vision_out.reshape(SLOTS * IMG_TOK, D_IN).astype(jnp.float32)
    average = lax.optimization_barrier(jnp.mean(inputs, axis=1, keepdims=True))
    centred = inputs - average
    inv_std = lax.rsqrt(lax.optimization_barrier(jnp.mean(centred * centred, axis=1, keepdims=True)) + epsilon)
    normed = centred * inv_std
    scaled = grad_rows * norm_gain
    input_grad = inv_std * (scaled - lax.optimization_barrier(jnp.mean(scaled, axis=1, keepdims=True)) - normed * lax.optimization_barrier(jnp.mean(scaled * normed, axis=1, keepdims=True)))
    norm_grads = jnp.stack([lax.optimization_barrier(jnp.sum(grad_rows * normed, axis=0)), lax.optimization_barrier(jnp.sum(grad_rows, axis=0))])
    branch = (input_grad.reshape(SLOTS * PATCH_IMG, DV) * layer_scale).astype(jnp.bfloat16)
    preact = hidden_pre.reshape(SLOTS * PATCH_IMG, FFV).astype(jnp.float32)
    activation, derivative = gelu_parts(preact)
    hidden_in = jnp.dot(branch, down_weight, preferred_element_type=jnp.float32)
    hidden_grad = (hidden_in * derivative).astype(jnp.bfloat16).reshape(SLOTS, PATCH_IMG, FFV)
    hidden_act = activation.astype(jnp.bfloat16)
    down_grad = lax.dot_general(branch, hidden_act, (((0,), (0,)), ((), ())), preferred_element_type=jnp.float32)
    return (hidden_grad, down_grad, norm_grads)
```

```python
import jax
import jax.numpy as jnp
from jax import lax
from jax.sharding import PartitionSpec as P

epsilon = 1e-06
half_root = 0.7071067811865476
inv_root_two_pi = 0.3989422804014327


def gelu_parts(preact):
    normal_cdf = 0.5 * (1.0 + jax.scipy.special.erf(preact * half_root))
    density = jnp.exp(-0.5 * preact * preact) * inv_root_two_pi
    return (preact * normal_cdf, normal_cdf + preact * density)


def owner_ranks(image_owner):
    positions = jnp.arange(image_owner.shape[0], dtype=jnp.int32)
    same_owner = (image_owner[:, None] == image_owner[None, :]) & (
        positions[None, :] < positions[:, None]
    )
    return jnp.sum(same_owner.astype(jnp.int32), axis=1)


def flat_norms(norm_terms):
    axes = ("node", "local")
    total = lax.axis_size("node") * lax.axis_size("local")
    width = norm_terms.shape[1]
    share = -(-width // total)
    padded = jnp.pad(norm_terms, ((0, 0), (0, share * total - width)))
    by_share = padded.reshape(2, total, share).transpose(1, 0, 2)
    terms = lax.all_to_all(by_share, axes, split_axis=0, concat_axis=0, tiled=True)
    sums = jnp.sum(terms, axis=0)
    whole = lax.all_gather(sums, axes, axis=0)
    return whole.transpose(1, 0, 2).reshape(2, total * share)[:, :width]


def body(
    upstream, block_image, image_owner, vision_out, norm_gain, layer_scale, down_weight, hidden_pre
):
    local_count = lax.axis_size("local")
    node_count = lax.axis_size("node")
    width_in = upstream.shape[1]
    model_width = layer_scale.shape[0]
    merge_count = width_in // model_width
    blocks_here = upstream.shape[0] // local_count
    node_blocks = local_count * blocks_here
    image_count = image_owner.shape[0]
    own_cap = vision_out.shape[0]
    unit_count = down_weight.shape[1]
    node_index = lax.axis_index("node")
    by_block = upstream.reshape(blocks_here, local_count, width_in)
    position_rows = lax.all_to_all(
        by_block, "local", split_axis=1, concat_axis=0, tiled=True
    ).reshape(node_blocks, width_in)
    image_table = jnp.arange(image_count, dtype=jnp.int32)
    block_match = block_image[:, None] == image_table[None, :]
    block_owner = jnp.sum(jnp.where(block_match, image_owner[None, :], 0), axis=1)
    block_rank = jnp.sum(jnp.where(block_match, owner_ranks(image_owner)[None, :], 0), axis=1)
    owner_table = block_owner.reshape(node_count, node_blocks)
    rank_table = block_rank.reshape(node_count, node_blocks)
    own_owners = lax.dynamic_index_in_dim(owner_table, node_index, 0, keepdims=False)
    node_table = jnp.arange(node_count, dtype=jnp.int32)
    to_owner = (node_table[:, None] == own_owners[None, :]).astype(jnp.bfloat16)
    node_sums = jnp.dot(to_owner, position_rows, preferred_element_type=jnp.float32).astype(
        jnp.bfloat16
    )
    arrived = lax.all_to_all(node_sums, "node", split_axis=0, concat_axis=0, tiled=True)
    from_owner = owner_table == node_index
    source_slot = jnp.max(jnp.where(from_owner, rank_table, -1), axis=1)
    slot_table = jnp.arange(own_cap, dtype=jnp.int32)
    slot_pick = (slot_table[:, None] == source_slot[None, :]).astype(jnp.bfloat16)
    grad_rows = jnp.dot(slot_pick, arrived, preferred_element_type=jnp.float32)
    inputs = vision_out.reshape(own_cap, width_in).astype(jnp.float32)
    average = jnp.mean(inputs, axis=1, keepdims=True)
    centred = inputs - average
    inv_std = lax.rsqrt(jnp.mean(centred * centred, axis=1, keepdims=True) + epsilon)
    normed = centred * inv_std
    scaled = grad_rows * norm_gain
    input_grad = inv_std * (
        scaled
        - jnp.mean(scaled, axis=1, keepdims=True)
        - normed * jnp.mean(scaled * normed, axis=1, keepdims=True)
    )
    norm_terms = jnp.stack([jnp.sum(grad_rows * normed, axis=0), jnp.sum(grad_rows, axis=0)])
    branch = (input_grad.reshape(own_cap, merge_count, model_width) * layer_scale).astype(
        jnp.bfloat16
    )
    patches = lax.all_gather(branch, "local", axis=1, tiled=True)
    patch_rows = patches.reshape(-1, model_width)
    row_count = patch_rows.shape[0]
    preact = hidden_pre.reshape(row_count, unit_count).astype(jnp.float32)
    activation, derivative = gelu_parts(preact)
    hidden_act = activation.astype(jnp.bfloat16)
    shard_rows = model_width // node_count
    hidden_in = jnp.dot(patch_rows, down_weight, preferred_element_type=jnp.float32)
    hidden_grad = (hidden_in * derivative).astype(jnp.bfloat16).reshape(hidden_pre.shape)
    by_column = patch_rows.reshape(row_count, node_count, shard_rows)
    my_columns = lax.all_to_all(by_column, "node", split_axis=1, concat_axis=0, tiled=True).reshape(
        node_count * row_count, shard_rows
    )
    down_grad = lax.dot_general(
        my_columns,
        lax.all_gather(hidden_act, "node", axis=0, tiled=True),
        (((0,), (0,)), ((), ())),
        preferred_element_type=jnp.float32,
    )
    norm_grads = flat_norms(norm_terms)
    return (hidden_grad, down_grad, norm_grads)


def solution(mesh):
    placed = (
        P(("node", "local"), None),
        P(),
        P(),
        P("node", "local", None),
        P(),
        P(),
        P(None, "local"),
        P("node", None, "local"),
    )
    return jax.shard_map(
        body,
        mesh=mesh,
        in_specs=placed,
        out_specs=(P("node", None, "local"), P("node", "local"), P()),
        check_vma=False,
    )
```

```python
import functools
import jax
import jax.numpy as jnp
from jax import lax
from jax.experimental import pallas as pl
from jax.experimental.pallas import tpu as pltpu
from jax.sharding import PartitionSpec as P

epsilon = 1e-06
half_root = 0.7071067811865476
inv_root_two_pi = 0.3989422804014327
MESH = pl.DeviceIdType.MESH


def gelu_parts(preact):
    normal_cdf = 0.5 * (1.0 + lax.erf(preact * half_root))
    density = jnp.exp(-0.5 * preact * preact) * inv_root_two_pi
    return (preact * normal_cdf, normal_cdf + preact * density)


def each(count, step):
    if count <= 8:
        for k in range(1, count):
            step(k)
    else:
        lax.fori_loop(1, count, lambda k, none: (step(k), none)[1], 0)


class Exchange:
    def __init__(self, axis, count, source, land, send_sem, recv_sem):
        self.axis, self.count, self.source, self.land = axis, count, source, land
        self.send_sem, self.recv_sem = send_sem, recv_sem
        self.me = lax.axis_index(axis)

    def copy(self, k):
        peer = lax.rem(self.me + k, self.count)
        return pltpu.make_async_remote_copy(
            src_ref=self.source(peer),
            dst_ref=self.land.at[self.me],
            send_sem=self.send_sem.at[k],
            recv_sem=self.recv_sem.at[k],
            device_id={self.axis: peer},
            device_id_type=MESH,
        )

    def start(self):
        each(self.count, lambda k: self.copy(k).start())

    def wait_recv(self):
        def one(k):
            origin = lax.rem(self.me + self.count - k, self.count)
            pltpu.make_async_remote_copy(
                src_ref=self.source(origin),
                dst_ref=self.land.at[origin],
                send_sem=self.send_sem.at[k],
                recv_sem=self.recv_sem.at[k],
                device_id={self.axis: origin},
                device_id_type=MESH,
            ).wait_recv()

        each(self.count, one)

    def wait_send(self):
        each(self.count, lambda k: self.copy(k).wait_send())


def kernel(
    sizes,
    up_ref, block_ref, owner_ref, vis_ref, gain_ref, scale_ref, weight_hbm, pre_ref,
    hid_ref, down_ref, norm_ref,
    slot_tab, up_f, send_a, land_a, send_b, land_b, normed_f, gain_f, grad_f,
    land_c, rows_x, land_d, land_act, pre_f, deriv_f, hid_f, acc_f, terms_f, norm_s, land_n1, sum_n, land_n2, land_n3,
    weight_v, weight_sem, sems_l, sems_n,
):
    nodes, locs, caps, merge, here, width, model, units, images, share, window, group = sizes
    node, loc = lax.axis_index("node"), lax.axis_index("local")
    blocks = locs * here
    row_count = locs * caps * merge
    columns = model // nodes
    f32, bf16 = jnp.float32, jnp.bfloat16

    weight_copy = pltpu.make_async_copy(weight_hbm, weight_v, weight_sem)
    weight_copy.start()

    barrier = pltpu.get_barrier_semaphore()

    def greet(axis, count, me):
        def one(k):
            pl.semaphore_signal(
                barrier, inc=1, device_id={axis: lax.rem(me + k, count)}, device_id_type=MESH
            )

        each(count, one)

    greet("local", locs, loc)
    greet("node", nodes, node)

    for b in range(here):
        for q in range(merge):
            part = up_ref[b * locs : (b + 1) * locs, q * model : (q + 1) * model].astype(f32)
            up_f[:, b * merge + q, :] = part
    send_a[...] = up_f[...].astype(bf16)
    land_a[pl.ds(loc, 1)] = send_a[pl.ds(loc, 1)]

    pl.semaphore_wait(barrier, locs + nodes - 2)
    move_a = Exchange("local", locs, lambda p: send_a.at[p], land_a, sems_l.at[0], sems_l.at[1])
    move_a.start()

    for t in range(locs):
        for s in range(caps):
            at = (t * caps + s) * merge
            pre_f[at : at + merge, :] = pre_ref[s, t * merge : (t + 1) * merge, :].astype(f32)
    activation, derivative = gelu_parts(pre_f[...])
    deriv_f[...] = derivative
    land_act[pl.ds(node, 1)] = activation.astype(bf16)[None]
    move_act = Exchange("node", nodes, lambda p: land_act.at[node], land_act, sems_n.at[0], sems_n.at[1])
    move_act.start()

    for q in range(merge):
        normed_f[:, q, :] = vis_ref[:, q * model : (q + 1) * model].astype(f32)
        gain_f[q : q + 1, :] = gain_ref[:, q * model : (q + 1) * model]
    count_in = 1.0 / width

    def mean(x):
        return jnp.sum(jnp.sum(x, axis=2, keepdims=True), axis=1, keepdims=True) * count_in

    inputs = normed_f[...]
    centred = inputs - mean(inputs)
    inv_std = lax.rsqrt(mean(centred * centred) + epsilon)
    normed_f[...] = centred * inv_std

    t_shape = (nodes * merge, blocks * merge)
    t_row = lax.broadcasted_iota(jnp.int32, t_shape, 0)
    t_col = lax.broadcasted_iota(jnp.int32, t_shape, 1)
    col_block = t_col // merge
    col_owner = jnp.full(t_shape, -1, jnp.int32)
    for b in range(blocks):
        owner = owner_ref[block_ref[node * blocks + b]]
        col_owner = jnp.where(col_block == b, owner, col_owner)
    to_owner = jnp.where(
        (t_row // merge == col_owner) & (t_row % merge == t_col % merge), 1.0, 0.0
    ).astype(bf16)

    taken = jnp.int32(0)
    for j in range(images):
        mine = owner_ref[j] == node
        slot_tab[j] = jnp.where(mine, taken, -1)
        taken = taken + jnp.where(mine, 1, 0)
    p_shape = (caps * merge, nodes * merge)
    p_row = lax.broadcasted_iota(jnp.int32, p_shape, 0)
    p_col = lax.broadcasted_iota(jnp.int32, p_shape, 1)
    col_node = p_col // merge

    def source(n, col_slot):
        slot = jnp.int32(-1)
        for b in range(blocks):
            slot = jnp.maximum(slot, slot_tab[block_ref[n * blocks + b]])
        return jnp.where(col_node == n, slot, col_slot)

    col_slot = jnp.full(p_shape, -1, jnp.int32)
    if nodes <= 8:
        for n in range(nodes):
            col_slot = source(n, col_slot)
    else:
        col_slot = lax.fori_loop(0, nodes, source, col_slot)
    pick = jnp.where(
        (p_row // merge == col_slot) & (p_row % merge == p_col % merge), 1.0, 0.0
    ).astype(bf16)

    move_a.wait_recv()
    arrived = land_a[...].astype(f32).reshape(blocks * merge, model).astype(bf16)
    sums = jnp.dot(to_owner, arrived, preferred_element_type=f32)
    send_b[...] = sums.reshape(nodes, merge, model).astype(bf16)
    move_b = Exchange("node", nodes, lambda p: send_b.at[p], land_b, sems_n.at[2], sems_n.at[3])
    move_b.start()
    land_b[pl.ds(node, 1)] = send_b[pl.ds(node, 1)]
    move_b.wait_recv()
    from_nodes = land_b[...].astype(f32).reshape(nodes * merge, model).astype(bf16)
    grad_f[...] = jnp.dot(pick, from_nodes, preferred_element_type=f32).reshape(caps, merge, model)

    grads = grad_f[...]
    normed = normed_f[...]
    scaled = grads * gain_f[...][None]
    input_grad = inv_std * (scaled - mean(scaled) - normed * mean(scaled * normed))
    branch = input_grad * scale_ref[...][None]
    land_c[pl.ds(loc, 1)] = branch.astype(bf16)[None]
    move_c = Exchange("local", locs, lambda p: land_c.at[loc], land_c, sems_l.at[2], sems_l.at[3])
    move_c.start()

    if share * locs > width:
        terms_f[:, width:] = jnp.zeros((2, share * locs - width), f32)
    gain_terms = jnp.sum(grads * normed, axis=0)
    bias_terms = jnp.sum(grads, axis=0)
    for q in range(merge):
        terms_f[0:1, q * model : (q + 1) * model] = gain_terms[q : q + 1, :]
        terms_f[1:2, q * model : (q + 1) * model] = bias_terms[q : q + 1, :]
    for t in range(locs):
        norm_s[t] = terms_f[:, t * share : (t + 1) * share]
    land_n1[pl.ds(loc, 1)] = norm_s[pl.ds(loc, 1)]
    move_n1 = Exchange("local", locs, lambda p: norm_s.at[p], land_n1, sems_l.at[4], sems_l.at[5])
    move_n1.start()

    move_c.wait_recv()
    rows_x[...] = land_c[...].astype(f32).reshape(row_count, model).astype(bf16)

    def window_at(n):
        low = jnp.minimum((n * columns) // 128, (model - window) // 128)
        return pl.multiple_of(low * 128, 128)

    move_d = Exchange(
        "node", nodes, lambda p: rows_x.at[:, pl.ds(window_at(p), window)], land_d, sems_n.at[4], sems_n.at[5]
    )
    move_d.start()
    land_d[pl.ds(node, 1)] = rows_x[:, pl.ds(window_at(node), window)][None]

    move_n1.wait_recv()
    sum_n[...] = jnp.sum(land_n1[...], axis=0)
    land_n2[pl.ds(node, 1)] = sum_n[...][None]
    move_n2 = Exchange("node", nodes, lambda p: sum_n, land_n2, sems_n.at[6], sems_n.at[7])
    move_n2.start()

    weight_copy.wait()
    hidden_in = lax.dot_general(
        rows_x[...], weight_v[...], (((1,), (1,)), ((), ())), preferred_element_type=f32
    )
    pre_f[...] = hidden_in * deriv_f[...]
    for t in range(locs):
        for s in range(caps):
            at = (t * caps + s) * merge
            hid_f[s, t * merge : (t + 1) * merge, :] = pre_f[at : at + merge, :]
    hid_ref[...] = hid_f[...].astype(bf16)

    move_n2.wait_recv()
    land_n3[pl.ds(loc, 1)] = jnp.sum(land_n2[...], axis=0)[None]
    move_n3 = Exchange("local", locs, lambda p: land_n3.at[loc], land_n3, sems_l.at[6], sems_l.at[7])
    move_n3.start()

    move_d.wait_recv()
    move_act.wait_recv()

    def product(first):
        left = land_d[pl.ds(first, group)].reshape(group * row_count, window)
        right = land_act[pl.ds(first, group)].reshape(group * row_count, units)
        return lax.dot_general(left, right, (((0,), (0,)), ((), ())), preferred_element_type=f32)

    acc_f[...] = product(0)
    if nodes > group:

        def more(g, none):
            acc_f[...] += product(g * group)
            return none

        lax.fori_loop(1, nodes // group, more, 0)
    skip = node * columns - window_at(node)
    if columns % 8 == 0:
        down_ref[...] = acc_f[pl.ds(pl.multiple_of(skip, 8), columns), :]
    else:
        down_ref[...] = pltpu.roll(acc_f[...], lax.rem(window - skip, window), 0)[:columns, :]

    move_n3.wait_recv()
    for t in range(locs):
        low, high = t * share, min((t + 1) * share, width)
        if high > low:
            norm_ref[:, low:high] = land_n3[t, :, : high - low]

    for move in (move_a, move_act, move_b, move_c, move_n1, move_d, move_n2, move_n3):
        move.wait_send()


def body(
    upstream, block_image, image_owner, vision_out, norm_gain, layer_scale, down_weight, hidden_pre
):
    locs = lax.axis_size("local")
    nodes = lax.axis_size("node")
    width = upstream.shape[1]
    model = layer_scale.shape[0]
    merge = width // model
    here = upstream.shape[0] // locs
    images = image_owner.shape[0]
    caps = vision_out.shape[0]
    units = down_weight.shape[1]
    columns = model // nodes
    row_count = locs * caps * merge
    share = -(-width // (locs * 128)) * 128
    window = max(
        -(-(n * columns + columns) // 128) * 128 - (n * columns) // 128 * 128 for n in range(nodes)
    )
    group = max(g for g in range(1, nodes + 1) if nodes % g == 0 and (g == 1 or g * row_count <= 512))
    sizes = (nodes, locs, caps, merge, here, width, model, units, images, share, window, group)
    f32, bf16 = jnp.float32, jnp.bfloat16
    vmem = pl.BlockSpec(memory_space=pltpu.VMEM)
    smem = pl.BlockSpec(memory_space=pltpu.SMEM)
    return pl.pallas_call(
        functools.partial(kernel, sizes),
        out_shape=(
            jax.ShapeDtypeStruct(hidden_pre.shape, bf16),
            jax.ShapeDtypeStruct((columns, units), f32),
            jax.ShapeDtypeStruct((2, width), f32),
        ),
        in_specs=[vmem, smem, smem, vmem, vmem, vmem, pl.BlockSpec(memory_space=pl.ANY), vmem],
        out_specs=(vmem, vmem, vmem),
        scratch_shapes=[
            pltpu.SMEM((images,), jnp.int32),
            pltpu.VMEM((locs, here * merge, model), f32),
            pltpu.VMEM((locs, here * merge, model), bf16),
            pltpu.VMEM((locs, here * merge, model), bf16),
            pltpu.VMEM((nodes, merge, model), bf16),
            pltpu.VMEM((nodes, merge, model), bf16),
            pltpu.VMEM((caps, merge, model), f32),
            pltpu.VMEM((merge, model), f32),
            pltpu.VMEM((caps, merge, model), f32),
            pltpu.VMEM((locs, caps, merge, model), bf16),
            pltpu.VMEM((row_count, model), bf16),
            pltpu.VMEM((nodes, row_count, window), bf16),
            pltpu.VMEM((nodes, row_count, units), bf16),
            pltpu.VMEM((row_count, units), f32),
            pltpu.VMEM((row_count, units), f32),
            pltpu.VMEM((caps, locs * merge, units), f32),
            pltpu.VMEM((window, units), f32),
            pltpu.VMEM((2, locs * share), f32),
            pltpu.VMEM((locs, 2, share), f32),
            pltpu.VMEM((locs, 2, share), f32),
            pltpu.VMEM((2, share), f32),
            pltpu.VMEM((nodes, 2, share), f32),
            pltpu.VMEM((locs, 2, share), f32),
            pltpu.VMEM((units, model), bf16),
            pltpu.SemaphoreType.DMA,
            pltpu.SemaphoreType.DMA((8, locs)),
            pltpu.SemaphoreType.DMA((8, nodes)),
        ],
        compiler_params=pltpu.CompilerParams(
            collective_id=0, has_side_effects=True, vmem_limit_bytes=56 * 1024 * 1024
        ),
    )(
        upstream,
        block_image,
        image_owner,
        vision_out.reshape(caps, width),
        norm_gain.reshape(1, width),
        layer_scale.reshape(1, model),
        down_weight.T,
        hidden_pre,
    )


def solution(mesh):
    placed = (
        P(("node", "local"), None),
        P(),
        P(),
        P("node", "local", None),
        P(),
        P(),
        P(None, "local"),
        P("node", None, "local"),
    )
    return jax.shard_map(
        body,
        mesh=mesh,
        in_specs=placed,
        out_specs=(P("node", None, "local"), P("node", "local"), P()),
        check_vma=False,
    )
```

```python
import functools
import jax
import jax.numpy as jnp
from jax import lax
from jax.experimental import pallas as pl
from jax.experimental.pallas import tpu as pltpu
from jax.sharding import PartitionSpec as P

epsilon = 1e-06
half_root = 0.7071067811865476
inv_root_two_pi = 0.3989422804014327
MESH = pl.DeviceIdType.MESH


def gelu_parts(preact):
    normal_cdf = 0.5 * (1.0 + lax.erf(preact * half_root))
    density = jnp.exp(-0.5 * preact * preact) * inv_root_two_pi
    return (preact * normal_cdf, normal_cdf + preact * density)


def each(count, step):
    if count <= 8:
        for k in range(1, count):
            step(k)
    else:
        lax.fori_loop(1, count, lambda k, none: (step(k), none)[1], 0)


class Exchange:
    def __init__(self, axis, count, source, land, send_sem, recv_sem):
        self.axis, self.count, self.source, self.land = axis, count, source, land
        self.send_sem, self.recv_sem = send_sem, recv_sem
        self.me = lax.axis_index(axis)

    def copy(self, k):
        peer = lax.rem(self.me + k, self.count)
        return pltpu.make_async_remote_copy(
            src_ref=self.source(peer),
            dst_ref=self.land.at[self.me],
            send_sem=self.send_sem.at[k],
            recv_sem=self.recv_sem.at[k],
            device_id={self.axis: peer},
            device_id_type=MESH,
        )

    def start(self):
        each(self.count, lambda k: self.copy(k).start())

    def wait_recv(self):
        def one(k):
            origin = lax.rem(self.me + self.count - k, self.count)
            pltpu.make_async_remote_copy(
                src_ref=self.source(origin),
                dst_ref=self.land.at[origin],
                send_sem=self.send_sem.at[k],
                recv_sem=self.recv_sem.at[k],
                device_id={self.axis: origin},
                device_id_type=MESH,
            ).wait_recv()

        each(self.count, one)

    def wait_send(self):
        each(self.count, lambda k: self.copy(k).wait_send())


def kernel(
    sizes,
    up_ref, block_ref, owner_ref, vis_ref, gain_hbm, scale_hbm, weight_hbm, pre_ref,
    hid_ref, down_ref, norm_ref,
    slot_tab, up_f, send_a, land_a, send_b, land_b, normed_f, gain_f, grad_f,
    land_c, rows_x, land_d, land_act, pre_f, deriv_f, hid_f, acc_f, terms_f, norm_s, land_n1, land_n2, land_n3,
    weight_v, scale_v, own_sems, sems_l, sems_n,
):
    nodes, locs, caps, merge, here, width, model, units, images, share, window, group = sizes
    node, loc = lax.axis_index("node"), lax.axis_index("local")
    blocks = locs * here
    row_count = locs * caps * merge
    columns = model // nodes
    f32, bf16 = jnp.float32, jnp.bfloat16

    weight_copy = pltpu.make_async_copy(weight_hbm, weight_v, own_sems.at[0])
    param_copies = [pltpu.make_async_copy(scale_hbm, scale_v.at[0], own_sems.at[1])]
    for q in range(merge):
        param_copies.append(
            pltpu.make_async_copy(
                gain_hbm.at[pl.ds(q * model, model)], gain_f.at[q], own_sems.at[2 + q]
            )
        )
    for copy in param_copies:
        copy.start()
    weight_copy.start()

    barrier = pltpu.get_barrier_semaphore()

    def greet(axis, count, me):
        def one(k):
            pl.semaphore_signal(
                barrier, inc=1, device_id={axis: lax.rem(me + k, count)}, device_id_type=MESH
            )

        each(count, one)

    greet("local", locs, loc)
    greet("node", nodes, node)

    for b in range(here):
        for q in range(merge):
            part = up_ref[b * locs : (b + 1) * locs, q * model : (q + 1) * model].astype(f32)
            up_f[:, b * merge + q, :] = part
    send_a[...] = up_f[...].astype(bf16)
    land_a[pl.ds(loc, 1)] = send_a[pl.ds(loc, 1)]

    pl.semaphore_wait(barrier, locs + nodes - 2)
    move_a = Exchange("local", locs, lambda p: send_a.at[p], land_a, sems_l.at[0], sems_l.at[1])
    move_a.start()

    for t in range(locs):
        for s in range(caps):
            at = (t * caps + s) * merge
            pre_f[at : at + merge, :] = pre_ref[s, t * merge : (t + 1) * merge, :].astype(f32)
    activation, derivative = gelu_parts(pre_f[...])
    deriv_f[...] = derivative
    land_act[pl.ds(node, 1)] = activation.astype(bf16)[None]
    move_act = Exchange("node", nodes, lambda p: land_act.at[node], land_act, sems_n.at[0], sems_n.at[1])
    move_act.start()

    for q in range(merge):
        normed_f[:, q, :] = vis_ref[:, q * model : (q + 1) * model].astype(f32)
    count_in = 1.0 / width

    def mean(x):
        return jnp.sum(jnp.sum(x, axis=2, keepdims=True), axis=1, keepdims=True) * count_in

    inputs = normed_f[...]
    centred = inputs - mean(inputs)
    inv_std = lax.rsqrt(mean(centred * centred) + epsilon)
    normed_f[...] = centred * inv_std

    t_shape = (nodes * merge, blocks * merge)
    t_row = lax.broadcasted_iota(jnp.int32, t_shape, 0)
    t_col = lax.broadcasted_iota(jnp.int32, t_shape, 1)
    col_block = t_col // merge
    col_owner = jnp.full(t_shape, -1, jnp.int32)
    for b in range(blocks):
        owner = owner_ref[block_ref[node * blocks + b]]
        col_owner = jnp.where(col_block == b, owner, col_owner)
    to_owner = jnp.where(
        (t_row // merge == col_owner) & (t_row % merge == t_col % merge), 1.0, 0.0
    ).astype(bf16)

    taken = jnp.int32(0)
    for j in range(images):
        mine = owner_ref[j] == node
        slot_tab[j] = jnp.where(mine, taken, -1)
        taken = taken + jnp.where(mine, 1, 0)
    p_shape = (caps * merge, nodes * merge)
    p_row = lax.broadcasted_iota(jnp.int32, p_shape, 0)
    p_col = lax.broadcasted_iota(jnp.int32, p_shape, 1)
    col_node = p_col // merge

    def source(n, col_slot):
        slot = jnp.int32(-1)
        for b in range(blocks):
            slot = jnp.maximum(slot, slot_tab[block_ref[n * blocks + b]])
        return jnp.where(col_node == n, slot, col_slot)

    col_slot = jnp.full(p_shape, -1, jnp.int32)
    if nodes <= 8:
        for n in range(nodes):
            col_slot = source(n, col_slot)
    else:
        col_slot = lax.fori_loop(0, nodes, source, col_slot)
    pick = jnp.where(
        (p_row // merge == col_slot) & (p_row % merge == p_col % merge), 1.0, 0.0
    ).astype(bf16)

    move_a.wait_recv()
    arrived = land_a[...].astype(f32).reshape(blocks * merge, model).astype(bf16)
    sums = jnp.dot(to_owner, arrived, preferred_element_type=f32)
    send_b[...] = sums.reshape(nodes, merge, model).astype(bf16)
    move_b = Exchange("node", nodes, lambda p: send_b.at[p], land_b, sems_n.at[2], sems_n.at[3])
    move_b.start()
    land_b[pl.ds(node, 1)] = send_b[pl.ds(node, 1)]
    move_b.wait_recv()
    from_nodes = land_b[...].astype(f32).reshape(nodes * merge, model).astype(bf16)
    grad_f[...] = jnp.dot(pick, from_nodes, preferred_element_type=f32).reshape(caps, merge, model)

    for copy in param_copies:
        copy.wait()
    grads = grad_f[...]
    normed = normed_f[...]
    scaled = grads * gain_f[...][None]
    input_grad = inv_std * (scaled - mean(scaled) - normed * mean(scaled * normed))
    branch = input_grad * scale_v[...][None]
    land_c[pl.ds(loc, 1)] = branch.astype(bf16)[None]
    move_c = Exchange("local", locs, lambda p: land_c.at[loc], land_c, sems_l.at[2], sems_l.at[3])
    move_c.start()

    if share * nodes > width:
        terms_f[:, width:] = jnp.zeros((2, share * nodes - width), f32)
    gain_terms = jnp.sum(grads * normed, axis=0)
    bias_terms = jnp.sum(grads, axis=0)
    for q in range(merge):
        terms_f[0:1, q * model : (q + 1) * model] = gain_terms[q : q + 1, :]
        terms_f[1:2, q * model : (q + 1) * model] = bias_terms[q : q + 1, :]
    for n in range(nodes):
        norm_s[n] = terms_f[:, n * share : (n + 1) * share]
    move_n1 = Exchange("node", nodes, lambda p: norm_s.at[p], land_n1, sems_n.at[6], sems_n.at[7])
    move_n1.start()
    land_n1[pl.ds(node, 1)] = norm_s[pl.ds(node, 1)]

    move_n1.wait_recv()
    land_n2[pl.ds(loc, 1)] = jnp.sum(land_n1[...], axis=0)[None]
    move_n2 = Exchange("local", locs, lambda p: land_n2.at[loc], land_n2, sems_l.at[4], sems_l.at[5])
    move_n2.start()

    move_c.wait_recv()
    rows_x[...] = land_c[...].astype(f32).reshape(row_count, model).astype(bf16)

    def window_at(n):
        low = jnp.minimum((n * columns) // 128, (model - window) // 128)
        return pl.multiple_of(low * 128, 128)

    move_d = Exchange(
        "node", nodes, lambda p: rows_x.at[:, pl.ds(window_at(p), window)], land_d, sems_n.at[4], sems_n.at[5]
    )
    move_d.start()
    land_d[pl.ds(node, 1)] = rows_x[:, pl.ds(window_at(node), window)][None]

    move_n2.wait_recv()
    land_n3[pl.ds(node, 1)] = jnp.sum(land_n2[...], axis=0)[None]
    move_n3 = Exchange("node", nodes, lambda p: land_n3.at[node], land_n3, sems_n.at[8], sems_n.at[9])
    move_n3.start()

    weight_copy.wait()
    hidden_in = lax.dot_general(
        rows_x[...], weight_v[...], (((1,), (1,)), ((), ())), preferred_element_type=f32
    )
    pre_f[...] = hidden_in * deriv_f[...]
    for t in range(locs):
        for s in range(caps):
            at = (t * caps + s) * merge
            hid_f[s, t * merge : (t + 1) * merge, :] = pre_f[at : at + merge, :]
    hid_ref[...] = hid_f[...].astype(bf16)

    move_d.wait_recv()
    move_act.wait_recv()

    def product(first):
        left = land_d[pl.ds(first, group)].reshape(group * row_count, window)
        right = land_act[pl.ds(first, group)].reshape(group * row_count, units)
        return lax.dot_general(left, right, (((0,), (0,)), ((), ())), preferred_element_type=f32)

    acc_f[...] = product(0)
    if nodes > group:

        def more(g, none):
            acc_f[...] += product(g * group)
            return none

        lax.fori_loop(1, nodes // group, more, 0)
    skip = node * columns - window_at(node)
    if columns % 8 == 0:
        down_ref[...] = acc_f[pl.ds(pl.multiple_of(skip, 8), columns), :]
    else:
        down_ref[...] = pltpu.roll(acc_f[...], lax.rem(window - skip, window), 0)[:columns, :]

    move_n3.wait_recv()
    for n in range(nodes):
        low, high = n * share, min((n + 1) * share, width)
        if high > low:
            norm_ref[:, low:high] = land_n3[n, :, : high - low]

    for move in (move_a, move_act, move_b, move_c, move_n1, move_d, move_n2, move_n3):
        move.wait_send()


def settle(*refs):
    copies = [pltpu.make_async_copy(refs[i], refs[3 + i], refs[6].at[i]) for i in range(3)]
    for copy in copies:
        copy.start()
    for copy in copies:
        copy.wait()


def body(
    upstream, block_image, image_owner, vision_out, norm_gain, layer_scale, down_weight, hidden_pre
):
    locs = lax.axis_size("local")
    nodes = lax.axis_size("node")
    width = upstream.shape[1]
    model = layer_scale.shape[0]
    merge = width // model
    here = upstream.shape[0] // locs
    images = image_owner.shape[0]
    caps = vision_out.shape[0]
    units = down_weight.shape[1]
    columns = model // nodes
    row_count = locs * caps * merge
    share = -(-width // (nodes * 128)) * 128
    window = max(
        -(-(n * columns + columns) // 128) * 128 - (n * columns) // 128 * 128 for n in range(nodes)
    )
    group = max(g for g in range(1, nodes + 1) if nodes % g == 0 and (g == 1 or g * row_count <= 512))
    sizes = (nodes, locs, caps, merge, here, width, model, units, images, share, window, group)
    f32, bf16 = jnp.float32, jnp.bfloat16
    vmem = pl.BlockSpec(memory_space=pltpu.VMEM)
    smem = pl.BlockSpec(memory_space=pltpu.SMEM)
    anywhere = pl.BlockSpec(memory_space=pl.ANY)
    shapes = (
        jax.ShapeDtypeStruct(hidden_pre.shape, bf16),
        jax.ShapeDtypeStruct((columns, units), f32),
        jax.ShapeDtypeStruct((2, width), f32),
    )
    results = pl.pallas_call(
        functools.partial(kernel, sizes),
        out_shape=shapes,
        in_specs=[vmem, smem, smem, vmem, anywhere, anywhere, anywhere, vmem],
        out_specs=(vmem, vmem, vmem),
        scratch_shapes=[
            pltpu.SMEM((images,), jnp.int32),
            pltpu.VMEM((locs, here * merge, model), f32),
            pltpu.VMEM((locs, here * merge, model), bf16),
            pltpu.VMEM((locs, here * merge, model), bf16),
            pltpu.VMEM((nodes, merge, model), bf16),
            pltpu.VMEM((nodes, merge, model), bf16),
            pltpu.VMEM((caps, merge, model), f32),
            pltpu.VMEM((merge, model), f32),
            pltpu.VMEM((caps, merge, model), f32),
            pltpu.VMEM((locs, caps, merge, model), bf16),
            pltpu.VMEM((row_count, model), bf16),
            pltpu.VMEM((nodes, row_count, window), bf16),
            pltpu.VMEM((nodes, row_count, units), bf16),
            pltpu.VMEM((row_count, units), f32),
            pltpu.VMEM((row_count, units), f32),
            pltpu.VMEM((caps, locs * merge, units), f32),
            pltpu.VMEM((window, units), f32),
            pltpu.VMEM((2, nodes * share), f32),
            pltpu.VMEM((nodes, 2, share), f32),
            pltpu.VMEM((nodes, 2, share), f32),
            pltpu.VMEM((locs, 2, share), f32),
            pltpu.VMEM((nodes, 2, share), f32),
            pltpu.VMEM((units, model), bf16),
            pltpu.VMEM((1, model), f32),
            pltpu.SemaphoreType.DMA((2 + merge,)),
            pltpu.SemaphoreType.DMA((6, locs)),
            pltpu.SemaphoreType.DMA((10, nodes)),
        ],
        compiler_params=pltpu.CompilerParams(
            collective_id=0, has_side_effects=True, vmem_limit_bytes=56 * 1024 * 1024
        ),
    )(
        upstream,
        block_image,
        image_owner,
        vision_out.reshape(caps, width),
        norm_gain,
        layer_scale,
        down_weight.T,
        hidden_pre,
    )
    return pl.pallas_call(
        settle,
        out_shape=shapes,
        in_specs=[anywhere] * 3,
        out_specs=(vmem,) * 3,
        scratch_shapes=[pltpu.SemaphoreType.DMA((3,))],
        compiler_params=pltpu.CompilerParams(vmem_limit_bytes=56 * 1024 * 1024),
    )(*results)


def solution(mesh):
    placed = (
        P(("node", "local"), None),
        P(),
        P(),
        P("node", "local", None),
        P(),
        P(),
        P(None, "local"),
        P("node", None, "local"),
    )
    return jax.shard_map(
        body,
        mesh=mesh,
        in_specs=placed,
        out_specs=(P("node", None, "local"), P("node", "local"), P()),
        check_vma=False,
    )
```

```python
import functools
import jax
import jax.numpy as jnp
from jax import lax
from jax.experimental import pallas as pl
from jax.experimental.pallas import tpu as pltpu
from jax.sharding import PartitionSpec as P

epsilon = 1e-06
half_root = 0.7071067811865476
inv_root_two_pi = 0.3989422804014327
MESH = pl.DeviceIdType.MESH


def gelu_parts(preact):
    normal_cdf = 0.5 * (1.0 + lax.erf(preact * half_root))
    density = jnp.exp(-0.5 * preact * preact) * inv_root_two_pi
    return (preact * normal_cdf, normal_cdf + preact * density)


def each(count, step):
    if count <= 8:
        for k in range(1, count):
            step(k)
    else:
        lax.fori_loop(1, count, lambda k, none: (step(k), none)[1], 0)


class Exchange:
    def __init__(self, axis, count, source, land, send_sem, recv_sem):
        self.axis, self.count, self.source = axis, count, source
        self.land = land if callable(land) else lambda slot: land.at[slot]
        self.send_sem, self.recv_sem = send_sem, recv_sem
        self.me = lax.axis_index(axis)

    def copy(self, k):
        peer = lax.rem(self.me + k, self.count)
        return pltpu.make_async_remote_copy(
            src_ref=self.source(peer),
            dst_ref=self.land(self.me),
            send_sem=self.send_sem.at[k],
            recv_sem=self.recv_sem.at[k],
            device_id={self.axis: peer},
            device_id_type=MESH,
        )

    def start(self):
        each(self.count, lambda k: self.copy(k).start())

    def wait_recv(self):
        def one(k):
            origin = lax.rem(self.me + self.count - k, self.count)
            pltpu.make_async_remote_copy(
                src_ref=self.source(origin),
                dst_ref=self.land(origin),
                send_sem=self.send_sem.at[k],
                recv_sem=self.recv_sem.at[k],
                device_id={self.axis: origin},
                device_id_type=MESH,
            ).wait_recv()

        each(self.count, one)

    def wait_send(self):
        each(self.count, lambda k: self.copy(k).wait_send())


def kernel(
    sizes,
    up_hbm, block_ref, owner_ref, vis_hbm, gain_hbm, scale_hbm, weight_hbm, pre_hbm,
    hid_ref, down_ref, norm_ref,
    slot_tab, up_f, send_a, land_a, send_b, land_b, normed_f, gain_f, grad_f,
    land_c, rows_x, land_d, land_act, pre_f, deriv_f, hid_f, acc_f, terms_f, norm_s, land_n1, land_n2, land_n3,
    weight_v, scale_v, up_ref, vis_ref, pre_ref, own_sems, sems_l, sems_n,
):
    nodes, locs, caps, merge, here, width, model, units, images, share, window, group, cut, early = sizes
    node, loc = lax.axis_index("node"), lax.axis_index("local")
    blocks = locs * here
    row_count = locs * caps * merge
    columns = model // nodes
    f32, bf16 = jnp.float32, jnp.bfloat16

    barrier = pltpu.get_barrier_semaphore()

    def greet(axis, count, me):
        def one(k):
            pl.semaphore_signal(
                barrier, inc=1, device_id={axis: lax.rem(me + k, count)}, device_id_type=MESH
            )

        each(count, one)

    greet("local", locs, loc)
    greet("node", nodes, node)

    weight_copy = pltpu.make_async_copy(weight_hbm, weight_v, own_sems.at[0])
    param_copies = [pltpu.make_async_copy(scale_hbm, scale_v.at[0], own_sems.at[1])]
    for q in range(merge):
        param_copies.append(
            pltpu.make_async_copy(
                gain_hbm.at[pl.ds(q * model, model)], gain_f.at[q], own_sems.at[2 + q]
            )
        )
    up_copy = pltpu.make_async_copy(up_hbm, up_ref, own_sems.at[2 + merge])
    pre_copy = pltpu.make_async_copy(pre_hbm, pre_ref, own_sems.at[3 + merge])
    vis_copy = pltpu.make_async_copy(vis_hbm, vis_ref, own_sems.at[4 + merge])
    up_copy.start()
    pre_copy.start()
    vis_copy.start()
    for copy in param_copies:
        copy.start()
    weight_copy.start()
    up_copy.wait()

    for b in range(here):
        for q in range(merge):
            part = up_ref[b * locs : (b + 1) * locs, q * model : (q + 1) * model].astype(f32)
            up_f[:, b * merge + q, :] = part
    send_a[...] = up_f[...].astype(bf16)
    land_a[pl.ds(loc, 1)] = send_a[pl.ds(loc, 1)]

    pl.semaphore_wait(barrier, locs + nodes - 2)
    move_a = Exchange("local", locs, lambda p: send_a.at[p], land_a, sems_l.at[0], sems_l.at[1])
    move_a.start()

    pre_copy.wait()
    for t in range(locs):
        for s in range(caps):
            at = (t * caps + s) * merge
            pre_f[at : at + merge, :] = pre_ref[s, t * merge : (t + 1) * merge, :].astype(f32)
    activation, derivative = gelu_parts(pre_f[...])
    deriv_f[...] = derivative
    land_act[pl.ds(node, 1)] = activation.astype(bf16)[None]
    move_act = Exchange("node", nodes, lambda p: land_act.at[node], land_act, sems_n.at[0], sems_n.at[1])
    move_act.start()

    vis_copy.wait()
    for q in range(merge):
        normed_f[:, q, :] = vis_ref[:, q * model : (q + 1) * model].astype(f32)
    count_in = 1.0 / width

    def mean(x):
        return jnp.sum(jnp.sum(x, axis=2, keepdims=True), axis=1, keepdims=True) * count_in

    inputs = normed_f[...]
    centred = inputs - mean(inputs)
    inv_std = lax.rsqrt(mean(centred * centred) + epsilon)
    normed_f[...] = centred * inv_std

    t_shape = (nodes * merge, blocks * merge)
    t_row = lax.broadcasted_iota(jnp.int32, t_shape, 0)
    t_col = lax.broadcasted_iota(jnp.int32, t_shape, 1)
    col_block = t_col // merge
    col_owner = jnp.full(t_shape, -1, jnp.int32)
    for b in range(blocks):
        owner = owner_ref[block_ref[node * blocks + b]]
        col_owner = jnp.where(col_block == b, owner, col_owner)
    to_owner = jnp.where(
        (t_row // merge == col_owner) & (t_row % merge == t_col % merge), 1.0, 0.0
    ).astype(bf16)

    taken = jnp.int32(0)
    for j in range(images):
        mine = owner_ref[j] == node
        slot_tab[j] = jnp.where(mine, taken, -1)
        taken = taken + jnp.where(mine, 1, 0)
    p_shape = (caps * merge, nodes * merge)
    p_row = lax.broadcasted_iota(jnp.int32, p_shape, 0)
    p_col = lax.broadcasted_iota(jnp.int32, p_shape, 1)
    col_node = p_col // merge

    def source(n, col_slot):
        slot = jnp.int32(-1)
        for b in range(blocks):
            slot = jnp.maximum(slot, slot_tab[block_ref[n * blocks + b]])
        return jnp.where(col_node == n, slot, col_slot)

    col_slot = jnp.full(p_shape, -1, jnp.int32)
    if nodes <= 8:
        for n in range(nodes):
            col_slot = source(n, col_slot)
    else:
        col_slot = lax.fori_loop(0, nodes, source, col_slot)
    pick = jnp.where(
        (p_row // merge == col_slot) & (p_row % merge == p_col % merge), 1.0, 0.0
    ).astype(bf16)

    move_a.wait_recv()
    arrived = land_a[...].astype(f32).reshape(blocks * merge, model).astype(bf16)
    sums = jnp.dot(to_owner, arrived, preferred_element_type=f32)
    send_b[...] = sums.reshape(nodes, merge, model).astype(bf16)
    move_b = Exchange("node", nodes, lambda p: send_b.at[p], land_b, sems_n.at[2], sems_n.at[3])
    move_b.start()
    land_b[pl.ds(node, 1)] = send_b[pl.ds(node, 1)]
    move_b.wait_recv()
    from_nodes = land_b[...].astype(f32).reshape(nodes * merge, model).astype(bf16)
    grad_f[...] = jnp.dot(pick, from_nodes, preferred_element_type=f32).reshape(caps, merge, model)

    grads = grad_f[...]
    normed = normed_f[...]
    if share * nodes > width:
        terms_f[:, width:] = jnp.zeros((2, share * nodes - width), f32)
    gain_terms = jnp.sum(grads * normed, axis=0)
    bias_terms = jnp.sum(grads, axis=0)
    for q in range(merge):
        terms_f[0:1, q * model : (q + 1) * model] = gain_terms[q : q + 1, :]
        terms_f[1:2, q * model : (q + 1) * model] = bias_terms[q : q + 1, :]
    for n in range(nodes):
        norm_s[n] = terms_f[:, n * share : (n + 1) * share]
    move_n1 = Exchange("node", nodes, lambda p: norm_s.at[p], land_n1, sems_n.at[6], sems_n.at[7])
    move_n1.start()
    land_n1[pl.ds(node, 1)] = norm_s[pl.ds(node, 1)]

    for copy in param_copies:
        copy.wait()
    scaled = grads * gain_f[...][None]
    input_grad = inv_std * (scaled - mean(scaled) - normed * mean(scaled * normed))
    branch = input_grad * scale_v[...][None]
    land_c[pl.ds(loc, 1)] = branch.astype(bf16)[None]

    def part(low, high):
        return lambda slot: land_c.at[slot, :, :, low:high]

    low_part, high_part = part(0, cut), part(cut, model)
    move_c = Exchange("local", locs, lambda p: low_part(loc), low_part, sems_l.at[2], sems_l.at[3])
    move_c.start()
    move_n1.wait_recv()
    land_n2[pl.ds(loc, 1)] = jnp.sum(land_n1[...], axis=0)[None]
    move_n2 = Exchange("local", locs, lambda p: land_n2.at[loc], land_n2, sems_l.at[4], sems_l.at[5])
    move_n2.start()
    move_e = Exchange("local", locs, lambda p: high_part(loc), high_part, sems_l.at[6], sems_l.at[7])
    move_e.start()

    def window_at(n):
        low = jnp.minimum((n * columns) // 128, (model - window) // 128)
        return pl.multiple_of(low * 128, 128)

    def copy_d(target, slot, n):
        return pltpu.make_async_remote_copy(
            src_ref=rows_x.at[:, pl.ds(window_at(target), window)],
            dst_ref=land_d.at[slot],
            send_sem=sems_n.at[4, target],
            recv_sem=sems_n.at[5, slot],
            device_id={"node": n},
            device_id_type=MESH,
        )

    def others(first, last, step):
        def one(n, none):
            @pl.when(n != node)
            def _():
                step(n)

            return none

        if last - first <= 8:
            for n in range(first, last):
                one(n, 0)
        else:
            lax.fori_loop(first, last, one, 0)

    def send_columns(n):
        copy_d(n, node, n).start()

    move_c.wait_recv()
    rows_x[:, :cut] = land_c[:, :, :, :cut].astype(f32).reshape(row_count, cut).astype(bf16)
    others(0, early, send_columns)

    move_n2.wait_recv()
    land_n3[pl.ds(node, 1)] = jnp.sum(land_n2[...], axis=0)[None]
    move_n3 = Exchange("node", nodes, lambda p: land_n3.at[node], land_n3, sems_n.at[8], sems_n.at[9])
    move_n3.start()

    move_e.wait_recv()
    rows_x[:, cut:] = land_c[:, :, :, cut:].astype(f32).reshape(row_count, model - cut).astype(bf16)
    others(early, nodes, send_columns)
    land_d[pl.ds(node, 1)] = rows_x[:, pl.ds(window_at(node), window)][None]

    weight_copy.wait()
    hidden_in = lax.dot_general(
        rows_x[...], weight_v[...], (((1,), (1,)), ((), ())), preferred_element_type=f32
    )
    pre_f[...] = hidden_in * deriv_f[...]
    for t in range(locs):
        for s in range(caps):
            at = (t * caps + s) * merge
            hid_f[s, t * merge : (t + 1) * merge, :] = pre_f[at : at + merge, :]
    hid_ref[...] = hid_f[...].astype(bf16)

    others(0, nodes, lambda n: copy_d(n, n, n).wait_recv())
    move_act.wait_recv()

    def product(first):
        left = land_d[pl.ds(first, group)].reshape(group * row_count, window)
        right = land_act[pl.ds(first, group)].reshape(group * row_count, units)
        return lax.dot_general(left, right, (((0,), (0,)), ((), ())), preferred_element_type=f32)

    acc_f[...] = product(0)
    if nodes > group:

        def more(g, none):
            acc_f[...] += product(g * group)
            return none

        lax.fori_loop(1, nodes // group, more, 0)
    skip = node * columns - window_at(node)
    if columns % 8 == 0:
        down_ref[...] = acc_f[pl.ds(pl.multiple_of(skip, 8), columns), :]
    else:
        down_ref[...] = pltpu.roll(acc_f[...], lax.rem(window - skip, window), 0)[:columns, :]

    move_n3.wait_recv()
    for n in range(nodes):
        low, high = n * share, min((n + 1) * share, width)
        if high > low:
            norm_ref[:, low:high] = land_n3[n, :, : high - low]

    for move in (move_a, move_act, move_b, move_c, move_e, move_n1, move_n2, move_n3):
        move.wait_send()
    others(0, nodes, lambda n: copy_d(n, node, n).wait_send())


def settle(*refs):
    copies = [pltpu.make_async_copy(refs[i], refs[3 + i], refs[6].at[i]) for i in range(3)]
    for copy in copies:
        copy.start()
    for copy in copies:
        copy.wait()


def body(
    upstream, block_image, image_owner, vision_out, norm_gain, layer_scale, down_weight, hidden_pre
):
    locs = lax.axis_size("local")
    nodes = lax.axis_size("node")
    width = upstream.shape[1]
    model = layer_scale.shape[0]
    merge = width // model
    here = upstream.shape[0] // locs
    images = image_owner.shape[0]
    caps = vision_out.shape[0]
    units = down_weight.shape[1]
    columns = model // nodes
    row_count = locs * caps * merge
    share = -(-width // (nodes * 128)) * 128
    window = max(
        -(-(n * columns + columns) // 128) * 128 - (n * columns) // 128 * 128 for n in range(nodes)
    )
    group = max(g for g in range(1, nodes + 1) if nodes % g == 0 and (g == 1 or g * row_count <= 512))
    cut = -(-model // 256) * 128
    starts = [min(n * columns // 128, (model - window) // 128) * 128 for n in range(nodes)]
    early = sum(1 for start in starts if start + window <= cut)
    sizes = (nodes, locs, caps, merge, here, width, model, units, images, share, window, group, cut, early)
    f32, bf16 = jnp.float32, jnp.bfloat16
    vmem = pl.BlockSpec(memory_space=pltpu.VMEM)
    smem = pl.BlockSpec(memory_space=pltpu.SMEM)
    anywhere = pl.BlockSpec(memory_space=pl.ANY)
    shapes = (
        jax.ShapeDtypeStruct(hidden_pre.shape, bf16),
        jax.ShapeDtypeStruct((columns, units), f32),
        jax.ShapeDtypeStruct((2, width), f32),
    )
    results = pl.pallas_call(
        functools.partial(kernel, sizes),
        out_shape=shapes,
        in_specs=[anywhere, smem, smem] + [anywhere] * 5,
        out_specs=(vmem, vmem, vmem),
        scratch_shapes=[
            pltpu.SMEM((images,), jnp.int32),
            pltpu.VMEM((locs, here * merge, model), f32),
            pltpu.VMEM((locs, here * merge, model), bf16),
            pltpu.VMEM((locs, here * merge, model), bf16),
            pltpu.VMEM((nodes, merge, model), bf16),
            pltpu.VMEM((nodes, merge, model), bf16),
            pltpu.VMEM((caps, merge, model), f32),
            pltpu.VMEM((merge, model), f32),
            pltpu.VMEM((caps, merge, model), f32),
            pltpu.VMEM((locs, caps, merge, model), bf16),
            pltpu.VMEM((row_count, model), bf16),
            pltpu.VMEM((nodes, row_count, window), bf16),
            pltpu.VMEM((nodes, row_count, units), bf16),
            pltpu.VMEM((row_count, units), f32),
            pltpu.VMEM((row_count, units), f32),
            pltpu.VMEM((caps, locs * merge, units), f32),
            pltpu.VMEM((window, units), f32),
            pltpu.VMEM((2, nodes * share), f32),
            pltpu.VMEM((nodes, 2, share), f32),
            pltpu.VMEM((nodes, 2, share), f32),
            pltpu.VMEM((locs, 2, share), f32),
            pltpu.VMEM((nodes, 2, share), f32),
            pltpu.VMEM((units, model), bf16),
            pltpu.VMEM((1, model), f32),
            pltpu.VMEM(upstream.shape, bf16),
            pltpu.VMEM((caps, width), bf16),
            pltpu.VMEM(hidden_pre.shape, bf16),
            pltpu.SemaphoreType.DMA((5 + merge,)),
            pltpu.SemaphoreType.DMA((8, locs)),
            pltpu.SemaphoreType.DMA((10, nodes)),
        ],
        compiler_params=pltpu.CompilerParams(
            collective_id=0, has_side_effects=True, vmem_limit_bytes=56 * 1024 * 1024
        ),
    )(
        upstream,
        block_image,
        image_owner,
        vision_out.reshape(caps, width),
        norm_gain,
        layer_scale,
        down_weight.T,
        hidden_pre,
    )
    return pl.pallas_call(
        settle,
        out_shape=shapes,
        in_specs=[anywhere] * 3,
        out_specs=(vmem,) * 3,
        scratch_shapes=[pltpu.SemaphoreType.DMA((3,))],
        compiler_params=pltpu.CompilerParams(vmem_limit_bytes=56 * 1024 * 1024),
    )(*results)


def solution(mesh):
    placed = (
        P(("node", "local"), None),
        P(),
        P(),
        P("node", "local", None),
        P(),
        P(),
        P(None, "local"),
        P("node", None, "local"),
    )
    return jax.shard_map(
        body,
        mesh=mesh,
        in_specs=placed,
        out_specs=(P("node", None, "local"), P("node", "local"), P()),
        check_vma=False,
    )
```

```python
import functools
import jax
import jax.numpy as jnp
from jax import lax
from jax.experimental import pallas as pl
from jax.experimental.pallas import tpu as pltpu
from jax.sharding import PartitionSpec as P

epsilon = 1e-06
half_root = 0.7071067811865476
inv_root_two_pi = 0.3989422804014327
MESH = pl.DeviceIdType.MESH


def gelu_parts(preact):
    normal_cdf = 0.5 * (1.0 + lax.erf(preact * half_root))
    density = jnp.exp(-0.5 * preact * preact) * inv_root_two_pi
    return (preact * normal_cdf, normal_cdf + preact * density)


def each(count, step):
    if count <= 8:
        for k in range(1, count):
            step(k)
    else:
        lax.fori_loop(1, count, lambda k, none: (step(k), none)[1], 0)


class Exchange:
    def __init__(self, axis, count, source, land, send_sem, recv_sem):
        self.axis, self.count, self.source = axis, count, source
        self.land = land if callable(land) else lambda slot: land.at[slot]
        self.send_sem, self.recv_sem = send_sem, recv_sem
        self.me = lax.axis_index(axis)

    def copy(self, k):
        peer = lax.rem(self.me + k, self.count)
        return pltpu.make_async_remote_copy(
            src_ref=self.source(peer),
            dst_ref=self.land(self.me),
            send_sem=self.send_sem.at[k],
            recv_sem=self.recv_sem.at[k],
            device_id={self.axis: peer},
            device_id_type=MESH,
        )

    def start(self):
        each(self.count, lambda k: self.copy(k).start())

    def wait_recv(self):
        def one(k):
            origin = lax.rem(self.me + self.count - k, self.count)
            pltpu.make_async_remote_copy(
                src_ref=self.source(origin),
                dst_ref=self.land(origin),
                send_sem=self.send_sem.at[k],
                recv_sem=self.recv_sem.at[k],
                device_id={self.axis: origin},
                device_id_type=MESH,
            ).wait_recv()

        each(self.count, one)

    def wait_send(self):
        each(self.count, lambda k: self.copy(k).wait_send())


def kernel(
    sizes,
    up_hbm, block_ref, owner_ref, vis_hbm, gain_hbm, scale_hbm, weight_hbm, pre_hbm,
    hid_ref, down_ref, norm_ref,
    slot_tab, up_f, send_a, land_a, send_b, land_b, normed_f, gain_f, grad_f,
    land_c, rows_x, land_d, land_act, pre_f, deriv_f, hid_f, acc_f, terms_f, norm_s, land_n1, land_n2, land_n3,
    weight_v, scale_v, up_ref, vis_ref, pre_ref, hid_v, norm_v, down_v, own_sems, sems_l, sems_n,
):
    nodes, locs, caps, merge, here, width, model, units, images, share, window, group, cut, early = sizes
    node, loc = lax.axis_index("node"), lax.axis_index("local")
    blocks = locs * here
    row_count = locs * caps * merge
    columns = model // nodes
    f32, bf16 = jnp.float32, jnp.bfloat16

    barrier = pltpu.get_barrier_semaphore()

    def greet(axis, count, me):
        def one(k):
            pl.semaphore_signal(
                barrier, inc=1, device_id={axis: lax.rem(me + k, count)}, device_id_type=MESH
            )

        each(count, one)

    greet("local", locs, loc)
    greet("node", nodes, node)

    weight_copy = pltpu.make_async_copy(weight_hbm, weight_v, own_sems.at[0])
    param_copies = [pltpu.make_async_copy(scale_hbm, scale_v.at[0], own_sems.at[1])]
    for q in range(merge):
        param_copies.append(
            pltpu.make_async_copy(
                gain_hbm.at[pl.ds(q * model, model)], gain_f.at[q], own_sems.at[2 + q]
            )
        )
    up_copy = pltpu.make_async_copy(up_hbm, up_ref, own_sems.at[2 + merge])
    pre_copy = pltpu.make_async_copy(pre_hbm, pre_ref, own_sems.at[3 + merge])
    vis_copy = pltpu.make_async_copy(vis_hbm, vis_ref, own_sems.at[4 + merge])
    up_copy.start()
    pre_copy.start()
    vis_copy.start()
    for copy in param_copies:
        copy.start()
    weight_copy.start()
    up_copy.wait()

    for b in range(here):
        for q in range(merge):
            part = up_ref[b * locs : (b + 1) * locs, q * model : (q + 1) * model].astype(f32)
            up_f[:, b * merge + q, :] = part
    send_a[...] = up_f[...].astype(bf16)
    land_a[pl.ds(loc, 1)] = send_a[pl.ds(loc, 1)]

    pl.semaphore_wait(barrier, locs + nodes - 2)
    move_a = Exchange("local", locs, lambda p: send_a.at[p], land_a, sems_l.at[0], sems_l.at[1])
    move_a.start()

    pre_copy.wait()
    for t in range(locs):
        for s in range(caps):
            at = (t * caps + s) * merge
            pre_f[at : at + merge, :] = pre_ref[s, t * merge : (t + 1) * merge, :].astype(f32)
    activation, derivative = gelu_parts(pre_f[...])
    deriv_f[...] = derivative
    land_act[pl.ds(node, 1)] = activation.astype(bf16)[None]
    move_act = Exchange("node", nodes, lambda p: land_act.at[node], land_act, sems_n.at[0], sems_n.at[1])
    move_act.start()

    vis_copy.wait()
    for q in range(merge):
        normed_f[:, q, :] = vis_ref[:, q * model : (q + 1) * model].astype(f32)
    count_in = 1.0 / width

    def mean(x):
        return jnp.sum(jnp.sum(x, axis=2, keepdims=True), axis=1, keepdims=True) * count_in

    inputs = normed_f[...]
    centred = inputs - mean(inputs)
    inv_std = lax.rsqrt(mean(centred * centred) + epsilon)
    normed_f[...] = centred * inv_std

    t_shape = (nodes * merge, blocks * merge)
    t_row = lax.broadcasted_iota(jnp.int32, t_shape, 0)
    t_col = lax.broadcasted_iota(jnp.int32, t_shape, 1)
    col_block = t_col // merge
    col_owner = jnp.full(t_shape, -1, jnp.int32)
    for b in range(blocks):
        owner = owner_ref[block_ref[node * blocks + b]]
        col_owner = jnp.where(col_block == b, owner, col_owner)
    to_owner = jnp.where(
        (t_row // merge == col_owner) & (t_row % merge == t_col % merge), 1.0, 0.0
    ).astype(bf16)

    taken = jnp.int32(0)
    for j in range(images):
        mine = owner_ref[j] == node
        slot_tab[j] = jnp.where(mine, taken, -1)
        taken = taken + jnp.where(mine, 1, 0)
    p_shape = (caps * merge, nodes * merge)
    p_row = lax.broadcasted_iota(jnp.int32, p_shape, 0)
    p_col = lax.broadcasted_iota(jnp.int32, p_shape, 1)
    col_node = p_col // merge

    def source(n, col_slot):
        slot = jnp.int32(-1)
        for b in range(blocks):
            slot = jnp.maximum(slot, slot_tab[block_ref[n * blocks + b]])
        return jnp.where(col_node == n, slot, col_slot)

    col_slot = jnp.full(p_shape, -1, jnp.int32)
    if nodes <= 8:
        for n in range(nodes):
            col_slot = source(n, col_slot)
    else:
        col_slot = lax.fori_loop(0, nodes, source, col_slot)
    pick = jnp.where(
        (p_row // merge == col_slot) & (p_row % merge == p_col % merge), 1.0, 0.0
    ).astype(bf16)

    move_a.wait_recv()
    arrived = land_a[...].astype(f32).reshape(blocks * merge, model).astype(bf16)
    sums = jnp.dot(to_owner, arrived, preferred_element_type=f32)
    send_b[...] = sums.reshape(nodes, merge, model).astype(bf16)
    move_b = Exchange("node", nodes, lambda p: send_b.at[p], land_b, sems_n.at[2], sems_n.at[3])
    move_b.start()
    land_b[pl.ds(node, 1)] = send_b[pl.ds(node, 1)]
    move_b.wait_recv()
    from_nodes = land_b[...].astype(f32).reshape(nodes * merge, model).astype(bf16)
    grad_f[...] = jnp.dot(pick, from_nodes, preferred_element_type=f32).reshape(caps, merge, model)

    grads = grad_f[...]
    normed = normed_f[...]
    for copy in param_copies:
        copy.wait()
    scaled = grads * gain_f[...][None]
    input_grad = inv_std * (scaled - mean(scaled) - normed * mean(scaled * normed))
    branch = input_grad * scale_v[...][None]
    land_c[pl.ds(loc, 1)] = branch.astype(bf16)[None]

    def part(low, high):
        return lambda slot: land_c.at[slot, :, :, low:high]

    low_part, high_part = part(0, cut), part(cut, model)
    move_c = Exchange("local", locs, lambda p: low_part(loc), low_part, sems_l.at[2], sems_l.at[3])
    move_c.start()

    if share * nodes > width:
        terms_f[:, width:] = jnp.zeros((2, share * nodes - width), f32)
    gain_terms = jnp.sum(grads * normed, axis=0)
    bias_terms = jnp.sum(grads, axis=0)
    for q in range(merge):
        terms_f[0:1, q * model : (q + 1) * model] = gain_terms[q : q + 1, :]
        terms_f[1:2, q * model : (q + 1) * model] = bias_terms[q : q + 1, :]
    for n in range(nodes):
        norm_s[n] = terms_f[:, n * share : (n + 1) * share]
    move_n1 = Exchange("node", nodes, lambda p: norm_s.at[p], land_n1, sems_n.at[6], sems_n.at[7])
    move_n1.start()
    land_n1[pl.ds(node, 1)] = norm_s[pl.ds(node, 1)]
    move_n1.wait_recv()
    land_n2[pl.ds(loc, 1)] = jnp.sum(land_n1[...], axis=0)[None]
    move_n2 = Exchange("local", locs, lambda p: land_n2.at[loc], land_n2, sems_l.at[4], sems_l.at[5])
    move_n2.start()
    move_e = Exchange("local", locs, lambda p: high_part(loc), high_part, sems_l.at[6], sems_l.at[7])
    move_e.start()

    def window_at(n):
        low = jnp.minimum((n * columns) // 128, (model - window) // 128)
        return pl.multiple_of(low * 128, 128)

    def copy_d(target, slot, n):
        return pltpu.make_async_remote_copy(
            src_ref=rows_x.at[:, pl.ds(window_at(target), window)],
            dst_ref=land_d.at[slot],
            send_sem=sems_n.at[4, target],
            recv_sem=sems_n.at[5, slot],
            device_id={"node": n},
            device_id_type=MESH,
        )

    def others(first, last, step):
        def one(n, none):
            @pl.when(n != node)
            def _():
                step(n)

            return none

        if last - first <= 8:
            for n in range(first, last):
                one(n, 0)
        else:
            lax.fori_loop(first, last, one, 0)

    def send_columns(n):
        copy_d(n, node, n).start()

    move_c.wait_recv()
    rows_x[:, :cut] = land_c[:, :, :, :cut].astype(f32).reshape(row_count, cut).astype(bf16)
    others(0, early, send_columns)

    move_n2.wait_recv()
    land_n3[pl.ds(node, 1)] = jnp.sum(land_n2[...], axis=0)[None]
    move_n3 = Exchange("node", nodes, lambda p: land_n3.at[node], land_n3, sems_n.at[8], sems_n.at[9])
    move_n3.start()

    move_e.wait_recv()
    rows_x[:, cut:] = land_c[:, :, :, cut:].astype(f32).reshape(row_count, model - cut).astype(bf16)
    others(early, nodes, send_columns)
    land_d[pl.ds(node, 1)] = rows_x[:, pl.ds(window_at(node), window)][None]

    weight_copy.wait()
    hidden_in = lax.dot_general(
        rows_x[...], weight_v[...], (((1,), (1,)), ((), ())), preferred_element_type=f32
    )
    pre_f[...] = hidden_in * deriv_f[...]
    for t in range(locs):
        for s in range(caps):
            at = (t * caps + s) * merge
            hid_f[s, t * merge : (t + 1) * merge, :] = pre_f[at : at + merge, :]
    hid_v[...] = hid_f[...].astype(bf16)
    hid_copy = pltpu.make_async_copy(hid_v, hid_ref, own_sems.at[5 + merge])
    hid_copy.start()

    move_n3.wait_recv()
    for n in range(nodes):
        low, high = n * share, min((n + 1) * share, width)
        if high > low:
            norm_v[:, low:high] = land_n3[n, :, : high - low]
    norm_copy = pltpu.make_async_copy(norm_v, norm_ref, own_sems.at[7 + merge])
    norm_copy.start()

    others(0, nodes, lambda n: copy_d(n, n, n).wait_recv())
    move_act.wait_recv()

    def product(first):
        left = land_d[pl.ds(first, group)].reshape(group * row_count, window)
        right = land_act[pl.ds(first, group)].reshape(group * row_count, units)
        return lax.dot_general(left, right, (((0,), (0,)), ((), ())), preferred_element_type=f32)

    acc_f[...] = product(0)
    if nodes > group:

        def more(g, none):
            acc_f[...] += product(g * group)
            return none

        lax.fori_loop(1, nodes // group, more, 0)
    skip = node * columns - window_at(node)
    if columns % 8 == 0:
        result = acc_f.at[pl.ds(pl.multiple_of(skip, 8), columns)]
    else:
        down_v[...] = pltpu.roll(acc_f[...], lax.rem(window - skip, window), 0)[:columns, :]
        result = down_v
    down_copy = pltpu.make_async_copy(result, down_ref, own_sems.at[6 + merge])
    down_copy.start()

    for move in (move_a, move_act, move_b, move_c, move_e, move_n1, move_n2, move_n3):
        move.wait_send()
    others(0, nodes, lambda n: copy_d(n, node, n).wait_send())
    for copy in (hid_copy, norm_copy, down_copy):
        copy.wait()


def settle(*refs):
    ins, outs, held, arrive, leave = refs[:3], refs[3:6], refs[6:9], refs[9], refs[10]
    copies = []
    for i in range(3):
        rows = ins[i].shape[0]
        step = -(-rows // 32) * 8 if rows > 64 else rows
        for low in range(0, rows, step):
            copies.append((i, slice(low, min(low + step, rows))))
    inward = [
        pltpu.make_async_copy(ins[i].at[part], held[i].at[part], arrive.at[c])
        for c, (i, part) in enumerate(copies)
    ]
    outward = [
        pltpu.make_async_copy(held[i].at[part], outs[i].at[part], leave.at[c])
        for c, (i, part) in enumerate(copies)
    ]
    for copy in inward:
        copy.start()
    for c in range(len(copies)):
        inward[c].wait()
        outward[c].start()
    for copy in outward:
        copy.wait()


def body(
    upstream, block_image, image_owner, vision_out, norm_gain, layer_scale, down_weight, hidden_pre
):
    locs = lax.axis_size("local")
    nodes = lax.axis_size("node")
    width = upstream.shape[1]
    model = layer_scale.shape[0]
    merge = width // model
    here = upstream.shape[0] // locs
    images = image_owner.shape[0]
    caps = vision_out.shape[0]
    units = down_weight.shape[1]
    columns = model // nodes
    row_count = locs * caps * merge
    share = -(-width // (nodes * 128)) * 128
    window = max(
        -(-(n * columns + columns) // 128) * 128 - (n * columns) // 128 * 128 for n in range(nodes)
    )
    group = max(g for g in range(1, nodes + 1) if nodes % g == 0 and (g == 1 or g * row_count <= 512))
    cut = -(-model // 256) * 128
    starts = [min(n * columns // 128, (model - window) // 128) * 128 for n in range(nodes)]
    early = sum(1 for start in starts if start + window <= cut)
    sizes = (nodes, locs, caps, merge, here, width, model, units, images, share, window, group, cut, early)
    f32, bf16 = jnp.float32, jnp.bfloat16
    vmem = pl.BlockSpec(memory_space=pltpu.VMEM)
    smem = pl.BlockSpec(memory_space=pltpu.SMEM)
    anywhere = pl.BlockSpec(memory_space=pl.ANY)
    shapes = (
        jax.ShapeDtypeStruct(hidden_pre.shape, bf16),
        jax.ShapeDtypeStruct((columns, units), f32),
        jax.ShapeDtypeStruct((2, width), f32),
    )
    results = pl.pallas_call(
        functools.partial(kernel, sizes),
        out_shape=shapes,
        in_specs=[anywhere, smem, smem] + [anywhere] * 5,
        out_specs=(anywhere,) * 3,
        scratch_shapes=[
            pltpu.SMEM((images,), jnp.int32),
            pltpu.VMEM((locs, here * merge, model), f32),
            pltpu.VMEM((locs, here * merge, model), bf16),
            pltpu.VMEM((locs, here * merge, model), bf16),
            pltpu.VMEM((nodes, merge, model), bf16),
            pltpu.VMEM((nodes, merge, model), bf16),
            pltpu.VMEM((caps, merge, model), f32),
            pltpu.VMEM((merge, model), f32),
            pltpu.VMEM((caps, merge, model), f32),
            pltpu.VMEM((locs, caps, merge, model), bf16),
            pltpu.VMEM((row_count, model), bf16),
            pltpu.VMEM((nodes, row_count, window), bf16),
            pltpu.VMEM((nodes, row_count, units), bf16),
            pltpu.VMEM((row_count, units), f32),
            pltpu.VMEM((row_count, units), f32),
            pltpu.VMEM((caps, locs * merge, units), f32),
            pltpu.VMEM((window, units), f32),
            pltpu.VMEM((2, nodes * share), f32),
            pltpu.VMEM((nodes, 2, share), f32),
            pltpu.VMEM((nodes, 2, share), f32),
            pltpu.VMEM((locs, 2, share), f32),
            pltpu.VMEM((nodes, 2, share), f32),
            pltpu.VMEM((units, model), bf16),
            pltpu.VMEM((1, model), f32),
            pltpu.VMEM(upstream.shape, bf16),
            pltpu.VMEM((caps, width), bf16),
            pltpu.VMEM(hidden_pre.shape, bf16),
            pltpu.VMEM(hidden_pre.shape, bf16),
            pltpu.VMEM((2, width), f32),
            pltpu.VMEM((columns, units) if columns % 8 else (8, 128), f32),
            pltpu.SemaphoreType.DMA((8 + merge,)),
            pltpu.SemaphoreType.DMA((8, locs)),
            pltpu.SemaphoreType.DMA((10, nodes)),
        ],
        compiler_params=pltpu.CompilerParams(
            collective_id=0, has_side_effects=True, vmem_limit_bytes=56 * 1024 * 1024
        ),
    )(
        upstream,
        block_image,
        image_owner,
        vision_out.reshape(caps, width),
        norm_gain,
        layer_scale,
        down_weight.T,
        hidden_pre,
    )
    return pl.pallas_call(
        settle,
        out_shape=shapes,
        in_specs=[anywhere] * 3,
        out_specs=(anywhere,) * 3,
        scratch_shapes=[pltpu.VMEM(shape.shape, shape.dtype) for shape in shapes]
        + [pltpu.SemaphoreType.DMA((16,)), pltpu.SemaphoreType.DMA((16,))],
        compiler_params=pltpu.CompilerParams(vmem_limit_bytes=56 * 1024 * 1024),
    )(*results)


def solution(mesh):
    placed = (
        P(("node", "local"), None),
        P(),
        P(),
        P("node", "local", None),
        P(),
        P(),
        P(None, "local"),
        P("node", None, "local"),
    )
    return jax.shard_map(
        body,
        mesh=mesh,
        in_specs=placed,
        out_specs=(P("node", None, "local"), P("node", "local"), P()),
        check_vma=False,
    )
```
